256 devices in a mesh: prow: 32 (over z, y_hi, core), pcol: 8 (over y_lo, x).
Axes of the slice: x: 4, y: 4 (y_hi: 2, y_lo: 2; y = y_hi * 2 + y_lo), z: 8, core: 2. Of those that a mesh axis runs over, the one named last changes fastest.
Arguments:
- struct_rows: int32 [2, 80], replicated, may hold values from 0 to 127, as said below
- lpanel: float32 [2, 24576, 192], P(None, 'prow'), may hold values from -0.046875 to 0.046875
- ainv: float32 [24576, 24576], P('prow', 'pcol'), may hold values from -6 to 6
- dinv: float32 [2, 192, 192], replicated, may hold values from -6 to 6
Outputs:
- inv_row: float32 [2, 192, 24576], P(None, None, 'pcol')
- inv_diag: float32 [2, 192, 192], replicated
The draws below stay inside these ranges and needn't reach their ends.
Inputs may be any that keep to these rules, and one draw needn't show every extreme that they name: `struct_rows`: each row lists 80 distinct block rows in increasing order; block rows 0 and 127 are always listed.
All inputs are finite; a program needn't handle non-finite values.
Results may differ from the reference program's by a relative error of at most 0.0001.
Values sent between devices are 32-bit elements; how exact they have to be, the bound alone decides.
No kernel may reach another device: no remote copies, remote signals or barrier semaphores. Data moves between devices by JAX's collectives and lax.ppermute only.
A program may use at most 64 MiB of HBM per device.

```python
import jax
import jax.numpy as jnp
from jax import lax

B = 192
NCOL = 2
NB = 128
S = 80


def draw_struct_rows(key, part):
    key = jax.random.fold_in(key, 11)
    blocks = jnp.arange(NB, dtype=jnp.int32)
    lists = []
    for column in range(NCOL):
        sub_key = jax.random.fold_in(key, column)
        ranks = jax.random.randint(sub_key, (NB,), 0, 2 * NB, dtype=jnp.int32) + blocks
        scores = ranks * NB + blocks
        scores = jnp.where(blocks == NB - 1, 4 * NB * NB, scores)
        scores = jnp.where(blocks == 0, 4 * NB * NB - 1, scores)
        _, chosen = lax.top_k(scores, S)
        lists.append(jnp.sort(chosen.astype(jnp.int32)))
    return jnp.stack(lists)


def block_scale(stream_key, dims, shards, smallest, largest):
    gain, own = 1.0, jax.random.fold_in(stream_key, 6)
    for axis_at, parts in shards:
        steps = jnp.exp(jax.random.uniform(jax.random.fold_in(own, axis_at), (parts,), jnp.float32, smallest / len(shards), largest / len(shards)))
        gain = gain * jnp.repeat(steps, dims[axis_at] // parts).reshape([-1 if axis == axis_at else 1 for axis in range(len(dims))])
    return gain


def bell_draw(key, extent, deviation, limit, shards=(), held_as=jnp.bfloat16):
    entries = jax.random.normal(key, extent, jnp.float32) * deviation
    if len(shards) > 0:
        entries = block_scale(key, extent, shards, -0.22, 0.18) * entries
    return jnp.clip(entries, min=-limit, max=limit).astype(held_as)


def setup_inputs(seed: int = 0) -> dict:
    arg_keys = jax.random.split(jax.random.key(seed), 5)
    return {
        "struct_rows": draw_struct_rows(jax.random.fold_in(arg_keys[4], 71), 0),
        "lpanel": bell_draw(arg_keys[1], (NCOL, NB * B, B), (S * B) ** -0.5, 0.046875, ((1, 32),), jnp.float32),
        "ainv": bell_draw(arg_keys[2], (NB * B, NB * B), 1.0, 6.0, ((0, 32), (1, 8)), jnp.float32),
        "dinv": bell_draw(arg_keys[3], (NCOL, B, B), 1.0, 6.0, (), jnp.float32),
    }


def reference(struct_rows, lpanel, ainv, dinv):
    blocks = jnp.arange(NB, dtype=jnp.int32)
    rows_out = []
    diags = []
    for column in range(NCOL):
        inside = jnp.any(struct_rows[column][:, None] == blocks[None, :], axis=0)
        row_mask = jnp.repeat(inside.astype(lpanel.dtype), B)
        masked = lpanel[column] * row_mask[:, None]
        inv_line = -jnp.dot(masked.T, ainv, precision=lax.Precision.HIGHEST, preferred_element_type=jnp.float32)
        inv_line = inv_line * row_mask[None, :]
        diag_block = dinv[column] - jnp.dot(inv_line, masked, precision=lax.Precision.HIGHEST, preferred_element_type=jnp.float32)
        rows_out.append(inv_line)
        diags.append(diag_block)
    return jnp.stack(rows_out), jnp.stack(diags)
```

```python
import functools

import jax
import jax.numpy as jnp
from jax import lax
from jax.experimental import pallas as pl
from jax.experimental.pallas import tpu as pltpu
from jax.sharding import PartitionSpec as P

AXES = ("prow", "pcol")
NZ, NYH, NC, NYL, NX = 8, 2, 2, 2, 4
REL = (4, 3, -3, 2, -2, 1, -1, 0)


def rank(z, yh, c, yl, x):
    return ((z * NYH + yh) * NC + c) * (NYL * NX) + yl * NX + x


def places():
    return [
        (z, yh, c, yl, x)
        for z in range(NZ)
        for yh in range(NYH)
        for c in range(NC)
        for yl in range(NYL)
        for x in range(NX)
    ]


def shift(value, dz=0, fz=0, fyh=0, fc=0, fyl=0, fx=0):
    perm = [
        (rank(z, yh, c, yl, x), rank(((z + dz) % NZ) ^ fz, yh ^ fyh, c ^ fc, yl ^ fyl, x ^ fx))
        for z, yh, c, yl, x in places()
    ]
    return lax.ppermute(value, AXES, perm)


def split(value):
    high = value.astype(jnp.bfloat16)
    low = (value - high.astype(jnp.float32)).astype(jnp.bfloat16)
    return high, low


def dot(a, b):
    return lax.dot_general(a, b, (((1,), (0,)), ((), ())), preferred_element_type=jnp.float32)


def product_kernel(meta, struct_ref, panel_ref, ainv_ref, out_ref, left_hl, left_h):
    width = out_ref.shape[1]

    @pl.when(pl.program_id(0) == 0)
    def _():
        listed = struct_ref[pl.ds(meta[0], 1), :]
        for i in range(panel_ref.shape[1] // width):
            hit = jnp.where(listed == meta[1] + i, -1.0, 0.0)
            sign = jnp.min(hit, axis=1, keepdims=True)
            block = (panel_ref[0, i * width : (i + 1) * width, :] * sign).T
            high, low = split(block)
            left_hl[:width, i * width : (i + 1) * width] = high
            left_hl[width:, i * width : (i + 1) * width] = low
            left_h[:, i * width : (i + 1) * width] = high

    high, low = split(ainv_ref[...])
    both = dot(left_hl[...], high)
    out_ref[0] = (both[width:] + dot(left_h[...], low)) + both[:width]


def product(meta, struct_rows, lpanel, ainv, first, count):
    _, rows, width = lpanel.shape
    cols = ainv.shape[1] // NZ
    return pl.pallas_call(
        product_kernel,
        out_shape=jax.ShapeDtypeStruct((count, width, cols), jnp.float32),
        grid_spec=pltpu.PrefetchScalarGridSpec(
            num_scalar_prefetch=1,
            grid=(count,),
            in_specs=[
                pl.BlockSpec(struct_rows.shape, lambda j, meta: (0, 0)),
                pl.BlockSpec((1, rows, width), lambda j, meta: (meta[0], 0, 0)),
                pl.BlockSpec((rows, cols), lambda j, meta: (0, meta[2 + first + j])),
            ],
            out_specs=pl.BlockSpec((1, width, cols), lambda j, meta: (j, 0, 0)),
            scratch_shapes=[
                pltpu.VMEM((2 * width, rows), jnp.bfloat16),
                pltpu.VMEM((width, rows), jnp.bfloat16),
            ],
        ),
        compiler_params=pltpu.CompilerParams(vmem_limit_bytes=24 * 1024 * 1024),
        cost_estimate=pl.CostEstimate(
            flops=6 * count * rows * width * cols, bytes_accessed=4 * count * rows * cols, transcendentals=0
        ),
    )(meta, struct_rows, lpanel, ainv)


def local(struct_rows, lpanel, ainv, dinv):
    row_index = lax.axis_index("prow")
    col_index = lax.axis_index("pcol")
    z = row_index // (NYH * NC)
    core = row_index % NC
    _, rows, width = lpanel.shape
    cols = ainv.shape[1]
    chunk = cols // NZ
    half = width // 2
    row_blocks = rows // width
    chunk_blocks = chunk // width
    owners = [(z + rel + NZ) % NZ for rel in REL]

    perm = []
    for pz, pyh, pc, pyl, px in places():
        q = pyl * NX + px
        z2, yh2, c2 = q >> 2, (q >> 1) & 1, q & 1
        dest_z = (pyh * NC + pc) * 2 + z2
        perm.append((rank(pz, pyh, pc, pyl, px), rank(dest_z, yh2, c2, pz // NX, pz % NX)))
    start = (col_index // 4) * chunk
    give = lax.dynamic_slice(lpanel, (col_index % 2, start, 0), (1, chunk, width))[0]
    facing = lax.ppermute(give, AXES, perm)

    def meta_of(k):
        return jnp.stack([k, row_index * row_blocks] + owners).astype(jnp.int32)

    other, own = meta_of(1 - core), meta_of(core)
    prod = functools.partial(product, struct_rows=struct_rows, lpanel=lpanel, ainv=ainv)
    cut = 3
    send_a = prod(other, first=0, count=cut)
    got_a = shift(send_a, fc=1)
    send_b = prod(other, first=cut, count=NZ - cut)
    got_b = shift(send_b, fc=1)
    own_a = prod(own, first=0, count=cut)
    own_b = prod(own, first=cut, count=NZ - cut)

    def part(rel):
        i = REL.index(rel)
        if i < cut:
            return own_a[i] + got_a[i]
        return own_b[i - cut] + got_b[i - cut]

    first = part(4)
    up = shift(first[:half], dz=1)
    down = shift(first[half:], dz=-1)
    p3, m3 = part(3), part(-3)
    send_up = jnp.concatenate([p3[:half] + up, p3[half:]])
    send_down = jnp.concatenate([m3[:half], m3[half:] + down])
    for d in (2, 1, 0):
        up = shift(send_up, dz=1)
        down = shift(send_down, dz=-1)
        if d:
            send_up = part(d) + up
            send_down = part(-d) + down
    mine = part(0) + up + down
    mine = mine + shift(mine, fyh=1)

    ids = (col_index * NZ + z) * chunk_blocks + jnp.arange(chunk_blocks, dtype=jnp.int32)
    listed = lax.dynamic_slice_in_dim(struct_rows, core, 1, 0)
    inside = jnp.any(listed[0][:, None] == ids[None, :], axis=0)
    col_mask = jnp.repeat(inside.astype(jnp.float32), width)
    mine = mine * col_mask[None, :]

    diag = lax.dot_general(
        mine, facing, (((1,), (0,)), ((), ())), precision=lax.Precision.HIGH, preferred_element_type=jnp.float32
    )

    held = [(mine, z)]
    up, down = mine, mine
    for step in (1, 2, 3):
        up = shift(up, dz=1)
        down = shift(down, dz=-1)
        held.append((up, (z - step + NZ) % NZ))
        held.append((down, (z + step) % NZ))
    up = shift(up[:half], dz=1)
    down = shift(down[half:], dz=-1)
    held.append((jnp.concatenate([up, down]), (z + 4) % NZ))

    inv_row = jnp.zeros((2, width, cols), jnp.float32)

    def put(out, value, k, owner):
        return lax.dynamic_update_slice(out, value[None], (k, 0, owner * chunk))

    for value, owner in held:
        inv_row = put(inv_row, value, core, owner)
    for group in (held[:3], held[3:5], held[5:7], held[7:]):
        got = shift(jnp.stack([value for value, _ in group]), fc=1)
        for i, (_, owner) in enumerate(group):
            inv_row = put(inv_row, got[i], 1 - core, owner)

    for move in (dict(fx=1), dict(fx=2), dict(fyl=1), dict(fz=1), dict(fz=2), dict(fz=4)):
        diag = diag + shift(diag, **move)
    diag_other = shift(diag, fc=1)
    pair = jnp.where(core == 0, jnp.stack([diag, diag_other]), jnp.stack([diag_other, diag]))
    return inv_row, dinv - pair


def solution(mesh):
    in_specs = (P(), P(None, "prow", None), P("prow", "pcol"), P())
    out_specs = (P(None, None, "pcol"), P())
    return jax.shard_map(local, mesh=mesh, in_specs=in_specs, out_specs=out_specs, check_vma=False)
```

```python
import functools

import jax
import jax.numpy as jnp
from jax import lax
from jax.experimental import pallas as pl
from jax.experimental.pallas import tpu as pltpu
from jax.sharding import PartitionSpec as P

AXES = ("prow", "pcol")
NZ, NYH, NC, NYL, NX = 8, 2, 2, 2, 4
SMALL = pl.CostEstimate(flops=1000, bytes_accessed=1000, transcendentals=0)


def rank(z, yh, c, yl, x):
    return ((z * NYH + yh) * NC + c) * (NYL * NX) + yl * NX + x


def places():
    return [
        (z, yh, c, yl, x)
        for z in range(NZ)
        for yh in range(NYH)
        for c in range(NC)
        for yl in range(NYL)
        for x in range(NX)
    ]


def shift(value, dz=0, fz=0, fyh=0, fc=0, fyl=0, fx=0):
    perm = [
        (rank(z, yh, c, yl, x), rank(((z + dz) % NZ) ^ fz, yh ^ fyh, c ^ fc, yl ^ fyl, x ^ fx))
        for z, yh, c, yl, x in places()
    ]
    return lax.ppermute(value, AXES, perm)


def ring(value):
    perm = [
        (rank(z, yh, c, yl, x), rank((z + 1 - 2 * c) % NZ, yh, c, yl, x)) for z, yh, c, yl, x in places()
    ]
    return lax.ppermute(value, AXES, perm)


def after(value, *others):
    return lax.optimization_barrier((value, *others))[0]


def split(value):
    high = value.astype(jnp.bfloat16)
    low = (value - high.astype(jnp.float32)).astype(jnp.bfloat16)
    return high, low


def dot(a, b):
    return lax.dot_general(a, b, (((1,), (0,)), ((), ())), preferred_element_type=jnp.float32)


def left_kernel(struct_hbm, panel_hbm, *refs):
    left, struct_v, panel_v, sems = refs[-4:]
    width = panel_v.shape[1]
    row_index = lax.axis_index("prow")
    core = row_index % NC
    loads = [
        pltpu.make_async_copy(struct_hbm, struct_v, sems.at[0]),
        pltpu.make_async_copy(panel_hbm, panel_v, sems.at[1]),
    ]
    for copy in loads:
        copy.start()
    for copy in loads:
        copy.wait()
    row_blocks = panel_v.shape[2] // width
    for k in range(2):
        column = core if k == 0 else 1 - core
        listed = struct_v[pl.ds(column, 1), :]
        for i in range(row_blocks):
            hit = jnp.where(listed == row_index * row_blocks + i, -1.0, 0.0)
            sign = jnp.min(hit, axis=1, keepdims=True)
            span = slice(i * width, (i + 1) * width)
            high, low = split(panel_v[column, :, span] * sign)
            left[k * width : (k + 1) * width, span] = high
            left[(2 + k) * width : (3 + k) * width, span] = low


def left_side(struct_rows, panel):
    _, width, rows = panel.shape
    hbm, vmem = pl.BlockSpec(memory_space=pltpu.HBM), pl.BlockSpec(memory_space=pltpu.VMEM)
    return pl.pallas_call(
        left_kernel,
        out_shape=jax.ShapeDtypeStruct((4 * width, rows), jnp.bfloat16),
        in_specs=[hbm, hbm],
        out_specs=vmem,
        scratch_shapes=[
            pltpu.VMEM(struct_rows.shape, jnp.int32),
            pltpu.VMEM(panel.shape, jnp.float32),
            pltpu.SemaphoreType.DMA((2,)),
        ],
        compiler_params=pltpu.CompilerParams(vmem_limit_bytes=14 * 1024 * 1024),
        cost_estimate=SMALL,
    )(struct_rows, panel)


def product_kernel(chunks, own_keep, other_keep, own_send, other_send, left, ainv_ref, *refs):
    keep_ref, send_ref = refs[-2:]
    _, width, cols = keep_ref.shape
    row_index = lax.axis_index("prow")
    z = row_index // (NYH * NC)
    way = 1 - 2 * (row_index % NC)
    for j in range(0, len(chunks), 2):
        some = chunks[j : j + 2]
        blocks = []
        for rel in some:
            owner = lax.rem(z + way * rel + NZ, NZ)
            blocks.append(ainv_ref[:, pl.ds(pl.multiple_of(owner * cols, 128), cols)])
        high, low = split(jnp.concatenate(blocks, axis=1))
        both = dot(left[...], high)
        total = (both[2 * width :] + dot(left[: 2 * width], low)) + both[: 2 * width]
        for i, rel in enumerate(some):
            own, other = (total[k * width : (k + 1) * width, i * cols : (i + 1) * cols] for k in (0, 1))
            if rel in own_keep:
                keep_ref[own_keep[rel]] = own
            if rel in other_keep:
                keep_ref[other_keep[rel]] = other
            if rel in own_send:
                send_ref[own_send[rel]] = own
            if rel in other_send:
                send_ref[other_send[rel]] = other


def product(chunks, own_keep, other_keep, own_send, other_send, ainv, left, wait_for=()):
    rows = ainv.shape[0]
    cols = ainv.shape[1] // NZ
    width = left.shape[0] // 4
    vmem, some = pl.BlockSpec(memory_space=pltpu.VMEM), pl.BlockSpec(memory_space=pl.ANY)
    outs = [
        jax.ShapeDtypeStruct((len(own_keep) + len(other_keep), width, cols), jnp.float32),
        jax.ShapeDtypeStruct((len(own_send) + len(other_send), width, cols), jnp.float32),
    ]
    return pl.pallas_call(
        functools.partial(product_kernel, chunks, own_keep, other_keep, own_send, other_send),
        out_shape=outs,
        in_specs=[vmem, vmem] + [some] * len(wait_for),
        out_specs=[vmem] * len(outs),
        compiler_params=pltpu.CompilerParams(vmem_limit_bytes=14 * 1024 * 1024),
        cost_estimate=SMALL,
    )(left, ainv, *wait_for)


def add_kernel(a_ref, b_ref, out_ref):
    out_ref[...] = a_ref[...] + b_ref[...]


def add(a, b):
    vmem = pl.BlockSpec(memory_space=pltpu.VMEM)
    return pl.pallas_call(
        add_kernel,
        out_shape=jax.ShapeDtypeStruct(a.shape, a.dtype),
        in_specs=[vmem, vmem],
        out_specs=vmem,
        cost_estimate=pl.CostEstimate(flops=0, bytes_accessed=2 * 10**7, transcendentals=0),
    )(a, b)


def put_kernel(pieces, has_out, *refs):
    sources = refs[: len(pieces)]
    out_ref, sems = refs[len(pieces) + has_out], refs[len(pieces) + has_out + 1]
    row_index = lax.axis_index("prow")
    z = row_index // (NYH * NC)
    core = row_index % NC
    way = 1 - 2 * core
    copies = []
    for ref, rels in zip(sources, pieces):
        cols = ref.shape[-1]
        for i, (other, rel) in enumerate(rels):
            column = 1 - core if other else core
            owner = lax.rem(z + way * rel + NZ, NZ)
            place = pl.ds(pl.multiple_of(owner * cols, 128), cols)
            block = ref if len(rels) == 1 else ref.at[i]
            copies.append(
                pltpu.make_async_copy(block.at[: out_ref.shape[1]], out_ref.at[column, :, place], sems.at[len(copies)])
            )
    for copy in copies:
        copy.start()
    for copy in copies:
        copy.wait()


def put(shape, values, pieces, out=None):
    count = sum(len(rels) for rels in pieces)
    operands = list(values) + ([] if out is None else [out])
    return pl.pallas_call(
        functools.partial(put_kernel, pieces, out is not None),
        out_shape=jax.ShapeDtypeStruct(shape, jnp.float32),
        in_specs=[pl.BlockSpec(memory_space=pltpu.VMEM)] * len(values)
        + [pl.BlockSpec(memory_space=pltpu.HBM)] * (len(operands) - len(values)),
        out_specs=pl.BlockSpec(memory_space=pltpu.HBM),
        scratch_shapes=[pltpu.SemaphoreType.DMA((count,))],
        input_output_aliases={} if out is None else {len(values): 0},
        cost_estimate=pl.CostEstimate(flops=0, bytes_accessed=count * 600000, transcendentals=0),
    )(*operands)


def local(struct_rows, lpanel, ainv, dinv):
    row_index = lax.axis_index("prow")
    col_index = lax.axis_index("pcol")
    z = row_index // (NYH * NC)
    core = row_index % NC
    panel = jnp.swapaxes(lpanel, 1, 2)
    _, width, rows = panel.shape
    cols = ainv.shape[1]
    chunk = cols // NZ
    chunk_blocks = chunk // width

    perm = []
    for pz, pyh, pc, pyl, px in places():
        dest_z = (pyh * NC + pc) * 2 + pyl
        perm.append((rank(pz, pyh, pc, pyl, px), rank(dest_z, px >> 1, px & 1, pz // NX, pz % NX)))
    give = lax.dynamic_slice(panel, (col_index % 2, 0, col_index // NX * chunk), (1, width, chunk))[0]
    facing = lax.ppermute(give, AXES, perm)

    left = left_side(struct_rows, panel)
    keep1, send1 = product((4, -3), {4: 0}, {}, {-3: 0}, {4: 1, -3: 2}, ainv, left)
    keep2, send2 = product((3, -2, -1), {3: 0}, {3: 1}, {-2: 0, -1: 1}, {-2: 2, -1: 3}, ainv, left)
    keep3, send3 = product((2, 1, 0), {2: 0, 1: 1, 0: 2}, {2: 3, 1: 4}, {}, {0: 0}, ainv, left)
    got1 = shift(after(send1, facing, keep2, keep3), fc=1)
    got2 = shift(send2, fc=1)
    got3 = shift(send3, fc=1)

    own_part = {
        4: keep1[0] + got1[1],
        3: keep2[0] + got1[2],
        2: keep3[0] + got2[2],
        1: keep3[1] + got2[3],
        0: keep3[2] + got3[0],
    }
    other_part = {3: keep2[1] + got1[0], 2: keep3[3] + got2[0], 1: keep3[4] + got2[1]}

    own_part = {rel: lax.optimization_barrier(value) for rel, value in own_part.items()}
    other_part = {rel: lax.optimization_barrier(value) for rel, value in other_part.items()}

    own_flow = ring(own_part[4])
    other_flow = ring(other_part[3])
    own_flow = ring(own_part[3] + own_flow)
    other_flow = ring(other_part[2] + other_flow)
    own_flow = ring(own_part[2] + own_flow)
    other_flow = ring(other_part[1] + other_flow)
    own_flow = ring(own_part[1] + own_flow)
    other_flow = shift(other_flow, fc=1)

    ids = (col_index * NZ + z) * chunk_blocks + jnp.arange(chunk_blocks, dtype=jnp.int32)
    listed = lax.dynamic_slice_in_dim(struct_rows, core, 1, 0)
    inside = jnp.any(listed[0][:, None] == ids[None, :], axis=0)
    col_mask = jnp.repeat(inside.astype(jnp.float32), width)[None, :]
    plane = ((own_part[0] + other_flow) + own_flow) * col_mask
    mine = add(plane, shift(plane, fyh=1))

    diag = lax.dot_general(
        plane, facing, (((1,), (1,)), ((), ())), precision=lax.Precision.HIGH, preferred_element_type=jnp.float32
    )
    x = col_index % NX
    quarter = width // NX

    def rows_of(j):
        return lax.dynamic_slice_in_dim(diag, (x ^ j) * quarter, quarter, 0)

    diag = rows_of(0) + sum(shift(rows_of(j), fx=j) for j in (1, 2, 3))
    over_y = [shift(diag, fyl=1), shift(diag, fyh=1), shift(diag, fyl=1, fyh=1)]

    def here(far):
        return ((False, -far),), ((True, -far),)

    def there(far):
        return ((True, far), (False, far))

    shape = (2, width, cols)

    own1 = ring(mine)
    own1, over_y = lax.optimization_barrier((own1, over_y))
    diag = diag + sum(over_y)
    tail = jnp.concatenate([diag[: quarter // 2], diag[quarter // 2 :]], axis=1)
    theirs = shift(mine, fc=1)
    other1 = ring(theirs)
    own2 = ring(jnp.concatenate([own1, tail]))
    other2 = ring(jnp.concatenate([other1, shift(tail, fc=1)]))
    there1 = shift(jnp.stack([own1, other1]), fc=1)
    own3 = ring(own2)
    other3 = ring(other2)
    there2 = shift(jnp.stack([own2[:width], other2[:width]]), fc=1)
    inv_row = put(shape, [mine, theirs, own1, other1, there1], [*here(0), *here(1), there(1)])
    own3, inv_row = lax.optimization_barrier((own3, inv_row))
    own4 = ring(own3)
    there3 = shift(jnp.stack([own3[:width], other3[:width]]), fc=1)
    inv_row = put(shape, [own2, other2, own3, other3, there2], [*here(2), *here(3), there(2)], inv_row)
    own4, inv_row = lax.optimization_barrier((own4, inv_row))
    last = ring(jnp.concatenate([own4[width:], other3[width:]]))
    there4 = shift(own4[:width], fc=1)
    inv_row = put(shape, [there3, own4, there4], [there(3), ((False, -4),), ((True, 4),)], inv_row)
    rows = tail.shape[0]
    own_sum = (tail + own2[width:]) + (own3[width:] + own4[width:]) + last[:rows]
    other_sum = (other2[width:] + other3[width:]) + last[rows:]
    from_there = shift(jnp.concatenate([other_sum, own_sum]), fc=1)
    own_sum, other_sum = own_sum + from_there[:rows], other_sum + from_there[rows:]
    both = jnp.where(core == 0, jnp.stack([own_sum, other_sum]), jnp.stack([other_sum, own_sum]))
    both = jnp.concatenate([both[:, :, :width], both[:, :, width:]], axis=1)
    over_x = [shift(both, fx=j) for j in (1, 2, 3)]
    inv_row, over_x = lax.optimization_barrier((inv_row, over_x))
    blocks = [both] + over_x
    blocks = [jnp.where(x % 2 == 0, blocks[j], blocks[j ^ 1]) for j in range(4)]
    blocks = [jnp.where(x < 2, blocks[j], blocks[j ^ 2]) for j in range(4)]
    total = jnp.concatenate(blocks, axis=1)
    return inv_row, dinv - total


def solution(mesh):
    in_specs = (P(), P(None, "prow", None), P("prow", "pcol"), P())
    out_specs = (P(None, None, "pcol"), P())
    return jax.shard_map(local, mesh=mesh, in_specs=in_specs, out_specs=out_specs, check_vma=False)
```

```python
import functools

import jax
import jax.numpy as jnp
from jax import lax
from jax.experimental import pallas as pl
from jax.experimental.pallas import tpu as pltpu
from jax.sharding import PartitionSpec as P

AXES = ("prow", "pcol")
NZ, NYH, NC, NYL, NX = 8, 2, 2, 2, 4
SMALL = pl.CostEstimate(flops=1000, bytes_accessed=1000, transcendentals=0)


def rank(z, yh, c, yl, x):
    return ((z * NYH + yh) * NC + c) * (NYL * NX) + yl * NX + x


def places():
    return [
        (z, yh, c, yl, x)
        for z in range(NZ)
        for yh in range(NYH)
        for c in range(NC)
        for yl in range(NYL)
        for x in range(NX)
    ]


def shift(value, dz=0, fz=0, fyh=0, fc=0, fyl=0, fx=0):
    perm = [
        (rank(z, yh, c, yl, x), rank(((z + dz) % NZ) ^ fz, yh ^ fyh, c ^ fc, yl ^ fyl, x ^ fx))
        for z, yh, c, yl, x in places()
    ]
    return lax.ppermute(value, AXES, perm)


def ring(value):
    perm = [
        (rank(z, yh, c, yl, x), rank((z + 1 - 2 * c) % NZ, yh, c, yl, x)) for z, yh, c, yl, x in places()
    ]
    return lax.ppermute(value, AXES, perm)


def after(value, *others):
    return lax.optimization_barrier((value, *others))[0]


def split(value):
    high = value.astype(jnp.bfloat16)
    low = (value - high.astype(jnp.float32)).astype(jnp.bfloat16)
    return high, low


def dot(a, b):
    return lax.dot_general(a, b, (((1,), (0,)), ((), ())), preferred_element_type=jnp.float32)


def left_kernel(struct_hbm, panel_hbm, *refs):
    left, struct_v, panel_v, sems = refs[-4:]
    width = panel_v.shape[1]
    row_index = lax.axis_index("prow")
    core = row_index % NC
    loads = [
        pltpu.make_async_copy(struct_hbm, struct_v, sems.at[0]),
        pltpu.make_async_copy(panel_hbm, panel_v, sems.at[1]),
    ]
    for copy in loads:
        copy.start()
    for copy in loads:
        copy.wait()
    row_blocks = panel_v.shape[2] // width
    for k in range(2):
        column = core if k == 0 else 1 - core
        listed = struct_v[pl.ds(column, 1), :]
        for i in range(row_blocks):
            hit = jnp.where(listed == row_index * row_blocks + i, -1.0, 0.0)
            sign = jnp.min(hit, axis=1, keepdims=True)
            span = slice(i * width, (i + 1) * width)
            high, low = split(panel_v[column, :, span] * sign)
            left[k * width : (k + 1) * width, span] = high
            left[(2 + k) * width : (3 + k) * width, span] = low


def left_side(struct_rows, panel):
    _, width, rows = panel.shape
    hbm, vmem = pl.BlockSpec(memory_space=pltpu.HBM), pl.BlockSpec(memory_space=pltpu.VMEM)
    return pl.pallas_call(
        left_kernel,
        out_shape=jax.ShapeDtypeStruct((4 * width, rows), jnp.bfloat16),
        in_specs=[hbm, hbm],
        out_specs=vmem,
        scratch_shapes=[
            pltpu.VMEM(struct_rows.shape, jnp.int32),
            pltpu.VMEM(panel.shape, jnp.float32),
            pltpu.SemaphoreType.DMA((2,)),
        ],
        compiler_params=pltpu.CompilerParams(vmem_limit_bytes=14 * 1024 * 1024),
        cost_estimate=SMALL,
    )(struct_rows, panel)


def product_kernel(chunks, own_keep, other_keep, own_send, other_send, left, ainv_ref, *refs):
    keep_ref, send_ref = refs[-2:]
    _, width, cols = keep_ref.shape
    row_index = lax.axis_index("prow")
    z = row_index // (NYH * NC)
    way = 1 - 2 * (row_index % NC)
    for j in range(0, len(chunks), 2):
        some = chunks[j : j + 2]
        blocks = []
        for rel in some:
            owner = lax.rem(z + way * rel + NZ, NZ)
            blocks.append(ainv_ref[:, pl.ds(pl.multiple_of(owner * cols, 128), cols)])
        high, low = split(jnp.concatenate(blocks, axis=1))
        both = dot(left[...], high)
        total = (both[2 * width :] + dot(left[: 2 * width], low)) + both[: 2 * width]
        for i, rel in enumerate(some):
            own, other = (total[k * width : (k + 1) * width, i * cols : (i + 1) * cols] for k in (0, 1))
            if rel in own_keep:
                keep_ref[own_keep[rel]] = own
            if rel in other_keep:
                keep_ref[other_keep[rel]] = other
            if rel in own_send:
                send_ref[own_send[rel]] = own
            if rel in other_send:
                send_ref[other_send[rel]] = other


def product(chunks, own_keep, other_keep, own_send, other_send, ainv, left, wait_for=()):
    rows = ainv.shape[0]
    cols = ainv.shape[1] // NZ
    width = left.shape[0] // 4
    vmem, some = pl.BlockSpec(memory_space=pltpu.VMEM), pl.BlockSpec(memory_space=pl.ANY)
    outs = [
        jax.ShapeDtypeStruct((len(own_keep) + len(other_keep), width, cols), jnp.float32),
        jax.ShapeDtypeStruct((len(own_send) + len(other_send), width, cols), jnp.float32),
    ]
    return pl.pallas_call(
        functools.partial(product_kernel, chunks, own_keep, other_keep, own_send, other_send),
        out_shape=outs,
        in_specs=[vmem, vmem] + [some] * len(wait_for),
        out_specs=[vmem] * len(outs),
        compiler_params=pltpu.CompilerParams(vmem_limit_bytes=14 * 1024 * 1024),
        cost_estimate=SMALL,
    )(left, ainv, *wait_for)


def add_kernel(a_ref, b_ref, out_ref):
    out_ref[...] = a_ref[...] + b_ref[...]


def add(a, b):
    vmem = pl.BlockSpec(memory_space=pltpu.VMEM)
    return pl.pallas_call(
        add_kernel,
        out_shape=jax.ShapeDtypeStruct(a.shape, a.dtype),
        in_specs=[vmem, vmem],
        out_specs=vmem,
        input_output_aliases={1: 0},
        compiler_params=pltpu.CompilerParams(vmem_limit_bytes=4 * 1024 * 1024),
        cost_estimate=pl.CostEstimate(flops=0, bytes_accessed=2 * 10**7, transcendentals=0),
    )(a, b)


def put_kernel(pieces, has_out, *refs):
    sources = refs[: len(pieces)]
    out_ref, sems = refs[len(pieces) + has_out], refs[len(pieces) + has_out + 1]
    row_index = lax.axis_index("prow")
    z = row_index // (NYH * NC)
    core = row_index % NC
    way = 1 - 2 * core
    copies = []
    for ref, rels in zip(sources, pieces):
        cols = ref.shape[-1]
        for i, (other, rel) in enumerate(rels):
            column = 1 - core if other else core
            owner = lax.rem(z + way * rel + NZ, NZ)
            place = pl.ds(pl.multiple_of(owner * cols, 128), cols)
            block = ref if len(rels) == 1 else ref.at[i]
            copies.append(
                pltpu.make_async_copy(block.at[: out_ref.shape[1]], out_ref.at[column, :, place], sems.at[len(copies)])
            )
    for copy in copies:
        copy.start()
    for copy in copies:
        copy.wait()


def put(shape, values, pieces, out=None):
    count = sum(len(rels) for rels in pieces)
    operands = list(values) + ([] if out is None else [out])
    return pl.pallas_call(
        functools.partial(put_kernel, pieces, out is not None),
        out_shape=jax.ShapeDtypeStruct(shape, jnp.float32),
        in_specs=[pl.BlockSpec(memory_space=pltpu.VMEM)] * len(values)
        + [pl.BlockSpec(memory_space=pltpu.HBM)] * (len(operands) - len(values)),
        out_specs=pl.BlockSpec(memory_space=pltpu.HBM),
        scratch_shapes=[pltpu.SemaphoreType.DMA((count,))],
        input_output_aliases={} if out is None else {len(values): 0},
        compiler_params=pltpu.CompilerParams(vmem_limit_bytes=8 * 1024 * 1024),
        cost_estimate=pl.CostEstimate(flops=0, bytes_accessed=count * 600000, transcendentals=0),
    )(*operands)


def local(struct_rows, lpanel, ainv, dinv):
    row_index = lax.axis_index("prow")
    col_index = lax.axis_index("pcol")
    z = row_index // (NYH * NC)
    core = row_index % NC
    panel = jnp.swapaxes(lpanel, 1, 2)
    _, width, rows = panel.shape
    cols = ainv.shape[1]
    chunk = cols // NZ
    chunk_blocks = chunk // width

    perm = []
    for pz, pyh, pc, pyl, px in places():
        dest_z = (pyh * NC + pc) * 2 + pyl
        perm.append((rank(pz, pyh, pc, pyl, px), rank(dest_z, px >> 1, px & 1, pz // NX, pz % NX)))
    give = lax.dynamic_slice(panel, (col_index % 2, 0, col_index // NX * chunk), (1, width, chunk))[0]
    facing = lax.ppermute(give, AXES, perm)

    left = left_side(struct_rows, panel)
    keep1, send1 = product((4, -3), {4: 0}, {}, {-3: 0}, {4: 1, -3: 2}, ainv, left)
    keep2, send2 = product((3, -2, -1), {3: 0}, {3: 1}, {-2: 0, -1: 1}, {-2: 2, -1: 3}, ainv, left)
    keep3, send3 = product((2, 1, 0), {2: 0, 1: 1, 0: 2}, {2: 3, 1: 4}, {}, {0: 0}, ainv, left)
    got1 = shift(after(send1, facing, keep2, keep3), fc=1)
    got2 = shift(send2, fc=1)
    got3 = shift(send3, fc=1)

    own_part = {
        4: keep1[0] + got1[1],
        3: keep2[0] + got1[2],
        2: keep3[0] + got2[2],
        1: keep3[1] + got2[3],
        0: keep3[2] + got3[0],
    }
    other_part = {3: keep2[1] + got1[0], 2: keep3[3] + got2[0], 1: keep3[4] + got2[1]}

    own_part = {rel: lax.optimization_barrier(value) for rel, value in own_part.items()}
    other_part = {rel: lax.optimization_barrier(value) for rel, value in other_part.items()}

    own_flow = ring(own_part[4])
    other_flow = ring(other_part[3])
    own_flow = ring(own_part[3] + own_flow)
    other_flow = ring(other_part[2] + other_flow)
    own_flow = ring(own_part[2] + own_flow)
    other_flow = ring(other_part[1] + other_flow)
    own_flow = ring(own_part[1] + own_flow)
    other_flow = shift(other_flow, fc=1)

    ids = (col_index * NZ + z) * chunk_blocks + jnp.arange(chunk_blocks, dtype=jnp.int32)
    listed = lax.dynamic_slice_in_dim(struct_rows, core, 1, 0)
    inside = jnp.any(listed[0][:, None] == ids[None, :], axis=0)
    col_mask = jnp.repeat(inside.astype(jnp.float32), width)[None, :]
    plane = ((own_part[0] + other_flow) + own_flow) * col_mask
    mine = add(plane, shift(plane, fyh=1))

    diag = lax.dot_general(
        plane, facing, (((1,), (1,)), ((), ())), precision=lax.Precision.HIGH, preferred_element_type=jnp.float32
    )
    x = col_index % NX
    quarter = width // NX

    def rows_of(j):
        return lax.dynamic_slice_in_dim(diag, (x ^ j) * quarter, quarter, 0)

    diag = rows_of(0) + sum(shift(rows_of(j), fx=j) for j in (1, 2, 3))
    over_y = [shift(diag, fyl=1), shift(diag, fyh=1), shift(diag, fyl=1, fyh=1)]

    def here(far):
        return ((False, -far),), ((True, -far),)

    def there(far):
        return ((True, far), (False, far))

    shape = (2, width, cols)

    own1 = ring(mine)
    own1, over_y = lax.optimization_barrier((own1, over_y))
    diag = diag + sum(over_y)
    tail = jnp.concatenate([diag[: quarter // 2], diag[quarter // 2 :]], axis=1)
    theirs = shift(mine, fc=1)
    other1 = ring(theirs)
    own2 = ring(jnp.concatenate([own1, tail]))
    other2 = ring(jnp.concatenate([other1, shift(tail, fc=1)]))
    there1 = shift(jnp.stack([own1, other1]), fc=1)
    own3 = ring(own2)
    other3 = ring(other2)
    there2 = shift(jnp.stack([own2[:width], other2[:width]]), fc=1)
    inv_row = put(shape, [mine, theirs, own1, other1, there1], [*here(0), *here(1), there(1)])
    own3, inv_row = lax.optimization_barrier((own3, inv_row))
    own4 = ring(own3)
    there3 = shift(jnp.stack([own3[:width], other3[:width]]), fc=1)
    inv_row = put(shape, [own2, other2, own3, other3, there2], [*here(2), *here(3), there(2)], inv_row)
    own4, inv_row = lax.optimization_barrier((own4, inv_row))
    last = ring(jnp.concatenate([own4[width:], other3[width:]]))
    there4 = shift(own4, fc=1)
    inv_row = put(shape, [there3, own4, there4], [there(3), ((False, -4),), ((True, 4),)], inv_row)
    rows = tail.shape[0]
    own_sum = (tail + own2[width:]) + (own3[width:] + own4[width:]) + last[:rows]
    other_sum = (other2[width:] + other3[width:]) + last[rows:]
    from_there = shift(jnp.concatenate([other_sum, own_sum]), fc=1)
    own_sum, other_sum = own_sum + from_there[:rows], other_sum + from_there[rows:]
    both = jnp.where(core == 0, jnp.stack([own_sum, other_sum]), jnp.stack([other_sum, own_sum]))
    both = jnp.concatenate([both[:, :, :width], both[:, :, width:]], axis=1)
    over_x = [shift(both, fx=j) for j in (1, 2, 3)]
    inv_row, over_x = lax.optimization_barrier((inv_row, over_x))
    blocks = [both] + over_x
    blocks = [jnp.where(x % 2 == 0, blocks[j], blocks[j ^ 1]) for j in range(4)]
    blocks = [jnp.where(x < 2, blocks[j], blocks[j ^ 2]) for j in range(4)]
    total = jnp.concatenate(blocks, axis=1)
    return inv_row, dinv - total


def solution(mesh):
    in_specs = (P(), P(None, "prow", None), P("prow", "pcol"), P())
    out_specs = (P(None, None, "pcol"), P())
    return jax.shard_map(local, mesh=mesh, in_specs=in_specs, out_specs=out_specs, check_vma=False)
```

```python
import functools

import jax
import jax.numpy as jnp
from jax import lax
from jax.experimental import pallas as pl
from jax.experimental.pallas import tpu as pltpu
from jax.sharding import PartitionSpec as P

AXES = ("prow", "pcol")
NZ, NYH, NC, NYL, NX = 8, 2, 2, 2, 4
SMALL = pl.CostEstimate(flops=1000, bytes_accessed=1000, transcendentals=0)


def rank(z, yh, c, yl, x):
    return ((z * NYH + yh) * NC + c) * (NYL * NX) + yl * NX + x


def places():
    return [
        (z, yh, c, yl, x)
        for z in range(NZ)
        for yh in range(NYH)
        for c in range(NC)
        for yl in range(NYL)
        for x in range(NX)
    ]


def shift(value, dz=0, fz=0, fyh=0, fc=0, fyl=0, fx=0):
    perm = [
        (rank(z, yh, c, yl, x), rank(((z + dz) % NZ) ^ fz, yh ^ fyh, c ^ fc, yl ^ fyl, x ^ fx))
        for z, yh, c, yl, x in places()
    ]
    return lax.ppermute(value, AXES, perm)


def ring(value):
    perm = [
        (rank(z, yh, c, yl, x), rank((z + 1 - 2 * c) % NZ, yh, c, yl, x)) for z, yh, c, yl, x in places()
    ]
    return lax.ppermute(value, AXES, perm)


def after(value, *others):
    return lax.optimization_barrier((value, *others))[0]


def split(value):
    high = value.astype(jnp.bfloat16)
    low = (value - high.astype(jnp.float32)).astype(jnp.bfloat16)
    return high, low


def dot(a, b):
    return lax.dot_general(a, b, (((1,), (0,)), ((), ())), preferred_element_type=jnp.float32)


def left_kernel(struct_hbm, panel_hbm, *refs):
    left, struct_v, panel_v, sems = refs[-4:]
    width = panel_v.shape[1]
    row_index = lax.axis_index("prow")
    core = row_index % NC
    loads = [
        pltpu.make_async_copy(struct_hbm, struct_v, sems.at[0]),
        pltpu.make_async_copy(panel_hbm, panel_v, sems.at[1]),
    ]
    for copy in loads:
        copy.start()
    for copy in loads:
        copy.wait()
    row_blocks = panel_v.shape[2] // width
    for k in range(2):
        column = core if k == 0 else 1 - core
        listed = struct_v[pl.ds(column, 1), :]
        for i in range(row_blocks):
            hit = jnp.where(listed == row_index * row_blocks + i, -1.0, 0.0)
            sign = jnp.min(hit, axis=1, keepdims=True)
            span = slice(i * width, (i + 1) * width)
            high, low = split(panel_v[column, :, span] * sign)
            left[k * width : (k + 1) * width, span] = high
            left[(2 + k) * width : (3 + k) * width, span] = low


def left_side(struct_rows, panel):
    _, width, rows = panel.shape
    hbm, vmem = pl.BlockSpec(memory_space=pltpu.HBM), pl.BlockSpec(memory_space=pltpu.VMEM)
    return pl.pallas_call(
        left_kernel,
        out_shape=jax.ShapeDtypeStruct((4 * width, rows), jnp.bfloat16),
        in_specs=[hbm, hbm],
        out_specs=vmem,
        scratch_shapes=[
            pltpu.VMEM(struct_rows.shape, jnp.int32),
            pltpu.VMEM(panel.shape, jnp.float32),
            pltpu.SemaphoreType.DMA((2,)),
        ],
        compiler_params=pltpu.CompilerParams(vmem_limit_bytes=14 * 1024 * 1024),
        cost_estimate=SMALL,
    )(struct_rows, panel)


def product_kernel(chunks, own_keep, other_keep, own_send, other_send, left, ainv_ref, *refs):
    keep_ref, send_ref = refs[-2:]
    _, width, cols = keep_ref.shape
    row_index = lax.axis_index("prow")
    z = row_index // (NYH * NC)
    way = 1 - 2 * (row_index % NC)
    for j in range(0, len(chunks), 2):
        some = chunks[j : j + 2]
        blocks = []
        for rel in some:
            owner = lax.rem(z + way * rel + NZ, NZ)
            blocks.append(ainv_ref[:, pl.ds(pl.multiple_of(owner * cols, 128), cols)])
        high, low = split(jnp.concatenate(blocks, axis=1))
        both = dot(left[...], high)
        total = (both[2 * width :] + dot(left[: 2 * width], low)) + both[: 2 * width]
        for i, rel in enumerate(some):
            own, other = (total[k * width : (k + 1) * width, i * cols : (i + 1) * cols] for k in (0, 1))
            if rel in own_keep:
                keep_ref[own_keep[rel]] = own
            if rel in other_keep:
                keep_ref[other_keep[rel]] = other
            if rel in own_send:
                send_ref[own_send[rel]] = own
            if rel in other_send:
                send_ref[other_send[rel]] = other


def product(chunks, own_keep, other_keep, own_send, other_send, ainv, left, wait_for=()):
    rows = ainv.shape[0]
    cols = ainv.shape[1] // NZ
    width = left.shape[0] // 4
    vmem, some = pl.BlockSpec(memory_space=pltpu.VMEM), pl.BlockSpec(memory_space=pl.ANY)
    outs = [
        jax.ShapeDtypeStruct((len(own_keep) + len(other_keep), width, cols), jnp.float32),
        jax.ShapeDtypeStruct((len(own_send) + len(other_send), width, cols), jnp.float32),
    ]
    return pl.pallas_call(
        functools.partial(product_kernel, chunks, own_keep, other_keep, own_send, other_send),
        out_shape=outs,
        in_specs=[vmem, vmem] + [some] * len(wait_for),
        out_specs=[vmem] * len(outs),
        compiler_params=pltpu.CompilerParams(vmem_limit_bytes=14 * 1024 * 1024),
        cost_estimate=SMALL,
    )(left, ainv, *wait_for)


def add_kernel(a_ref, b_ref, out_ref):
    out_ref[...] = a_ref[...] + b_ref[...]


def add(a, b):
    vmem = pl.BlockSpec(memory_space=pltpu.VMEM)
    return pl.pallas_call(
        add_kernel,
        out_shape=jax.ShapeDtypeStruct(a.shape, a.dtype),
        in_specs=[vmem, vmem],
        out_specs=vmem,
        input_output_aliases={1: 0},
        compiler_params=pltpu.CompilerParams(vmem_limit_bytes=4 * 1024 * 1024),
        cost_estimate=pl.CostEstimate(flops=0, bytes_accessed=2 * 10**7, transcendentals=0),
    )(a, b)


def put_kernel(pieces, has_out, *refs):
    sources = refs[: len(pieces)]
    out_ref, sems = refs[len(pieces) + has_out], refs[len(pieces) + has_out + 1]
    row_index = lax.axis_index("prow")
    z = row_index // (NYH * NC)
    core = row_index % NC
    way = 1 - 2 * core
    copies = []
    for ref, rels in zip(sources, pieces):
        cols = ref.shape[-1]
        for i, (other, rel) in enumerate(rels):
            column = 1 - core if other else core
            owner = lax.rem(z + way * rel + NZ, NZ)
            place = pl.ds(pl.multiple_of(owner * cols, 128), cols)
            block = ref if len(rels) == 1 else ref.at[i]
            copies.append(
                pltpu.make_async_copy(block.at[: out_ref.shape[1]], out_ref.at[column, :, place], sems.at[len(copies)])
            )
    for copy in copies:
        copy.start()
    for copy in copies:
        copy.wait()


def put(shape, values, pieces, out=None):
    count = sum(len(rels) for rels in pieces)
    operands = list(values) + ([] if out is None else [out])
    return pl.pallas_call(
        functools.partial(put_kernel, pieces, out is not None),
        out_shape=jax.ShapeDtypeStruct(shape, jnp.float32),
        in_specs=[pl.BlockSpec(memory_space=pltpu.VMEM)] * len(values)
        + [pl.BlockSpec(memory_space=pltpu.HBM)] * (len(operands) - len(values)),
        out_specs=pl.BlockSpec(memory_space=pltpu.HBM),
        scratch_shapes=[pltpu.SemaphoreType.DMA((count,))],
        input_output_aliases={} if out is None else {len(values): 0},
        compiler_params=pltpu.CompilerParams(vmem_limit_bytes=8 * 1024 * 1024),
        cost_estimate=pl.CostEstimate(flops=0, bytes_accessed=count * 600000, transcendentals=0),
    )(*operands)


def local(struct_rows, lpanel, ainv, dinv):
    row_index = lax.axis_index("prow")
    col_index = lax.axis_index("pcol")
    z = row_index // (NYH * NC)
    core = row_index % NC
    panel = jnp.swapaxes(lpanel, 1, 2)
    _, width, rows = panel.shape
    cols = ainv.shape[1]
    chunk = cols // NZ
    chunk_blocks = chunk // width

    perm = []
    for pz, pyh, pc, pyl, px in places():
        dest_z = (pyh * NC + pc) * 2 + pyl
        perm.append((rank(pz, pyh, pc, pyl, px), rank(dest_z, px >> 1, px & 1, pz // NX, pz % NX)))
    give = lax.dynamic_slice(panel, (col_index % 2, 0, col_index // NX * chunk), (1, width, chunk))[0]
    facing = lax.ppermute(give, AXES, perm)

    left = left_side(struct_rows, panel)
    keep1, send1 = product((4, -3), {4: 0}, {}, {-3: 0}, {4: 1, -3: 2}, ainv, left)
    keep2, send2 = product((3, -2, -1), {3: 0}, {3: 1}, {-2: 0, -1: 1}, {-2: 2, -1: 3}, ainv, left)
    keep3, send3 = product((2, 1, 0), {2: 0, 1: 1, 0: 2}, {2: 3, 1: 4}, {}, {0: 0}, ainv, left)
    far_own = shift(after(send1[1], facing, keep2, keep3), fc=1)
    got1 = shift(jnp.stack([send1[0], send1[2]]), fc=1)
    got2 = shift(send2, fc=1)
    got3 = shift(send3, fc=1)

    own_part = {
        4: keep1[0] + far_own,
        3: keep2[0] + got1[1],
        2: keep3[0] + got2[2],
        1: keep3[1] + got2[3],
        0: keep3[2] + got3[0],
    }
    other_part = {3: keep2[1] + got1[0], 2: keep3[3] + got2[0], 1: keep3[4] + got2[1]}

    own_part = {rel: lax.optimization_barrier(value) for rel, value in own_part.items()}
    other_part = {rel: lax.optimization_barrier(value) for rel, value in other_part.items()}

    own_flow = ring(own_part[4])
    other_flow = ring(other_part[3])
    own_flow = ring(own_part[3] + own_flow)
    other_flow = ring(other_part[2] + other_flow)
    own_flow = ring(own_part[2] + own_flow)
    other_flow = ring(other_part[1] + other_flow)
    own_flow = ring(own_part[1] + own_flow)
    other_flow = shift(other_flow, fc=1)

    ids = (col_index * NZ + z) * chunk_blocks + jnp.arange(chunk_blocks, dtype=jnp.int32)
    listed = lax.dynamic_slice_in_dim(struct_rows, core, 1, 0)
    inside = jnp.any(listed[0][:, None] == ids[None, :], axis=0)
    col_mask = jnp.repeat(inside.astype(jnp.float32), width)[None, :]
    plane = ((own_part[0] + other_flow) + own_flow) * col_mask
    mine = add(plane, shift(plane, fyh=1))

    diag = lax.dot_general(
        plane, facing, (((1,), (1,)), ((), ())), precision=lax.Precision.HIGH, preferred_element_type=jnp.float32
    )
    x = col_index % NX
    quarter = width // NX

    def rows_of(j):
        return lax.dynamic_slice_in_dim(diag, (x ^ j) * quarter, quarter, 0)

    diag = rows_of(0) + sum(shift(rows_of(j), fx=j) for j in (1, 2, 3))
    over_y = [shift(diag, fyl=1), shift(diag, fyh=1), shift(diag, fyl=1, fyh=1)]

    def here(far):
        return ((False, -far),), ((True, -far),)

    def there(far):
        return ((True, far), (False, far))

    shape = (2, width, cols)

    own1 = ring(mine)
    own1, over_y = lax.optimization_barrier((own1, over_y))
    diag = diag + sum(over_y)
    tail = jnp.concatenate([diag[: quarter // 2], diag[quarter // 2 :]], axis=1)
    theirs = shift(mine, fc=1)
    other1 = ring(theirs)
    own2 = ring(jnp.concatenate([own1, tail]))
    other2 = ring(jnp.concatenate([other1, shift(tail, fc=1)]))
    there1 = shift(jnp.stack([own1, other1]), fc=1)
    own3 = ring(own2)
    other3 = ring(other2)
    there2 = shift(jnp.stack([own2[:width], other2[:width]]), fc=1)
    inv_row = put(shape, [mine, theirs, own1, other1, there1], [*here(0), *here(1), there(1)])
    own3, inv_row = lax.optimization_barrier((own3, inv_row))
    own4 = ring(own3)
    there3 = shift(jnp.stack([own3[:width], other3[:width]]), fc=1)
    inv_row = put(shape, [own2, other2, own3, other3, there2], [*here(2), *here(3), there(2)], inv_row)
    own4, inv_row = lax.optimization_barrier((own4, inv_row))
    last = ring(jnp.concatenate([own4[width:], other3[width:]]))
    there4 = shift(own4, fc=1)
    inv_row = put(shape, [there3, own4, there4], [there(3), ((False, -4),), ((True, 4),)], inv_row)
    rows = tail.shape[0]
    own_sum = (tail + own2[width:]) + (own3[width:] + own4[width:]) + last[:rows]
    other_sum = (other2[width:] + other3[width:]) + last[rows:]
    from_there = shift(jnp.concatenate([other_sum, own_sum]), fc=1)
    own_sum, other_sum = own_sum + from_there[:rows], other_sum + from_there[rows:]
    both = jnp.where(core == 0, jnp.stack([own_sum, other_sum]), jnp.stack([other_sum, own_sum]))
    both = jnp.concatenate([both[:, :, :width], both[:, :, width:]], axis=1)
    over_x = [shift(both, fx=j) for j in (1, 2, 3)]
    inv_row, over_x = lax.optimization_barrier((inv_row, over_x))
    blocks = [both] + over_x
    blocks = [jnp.where(x % 2 == 0, blocks[j], blocks[j ^ 1]) for j in range(4)]
    blocks = [jnp.where(x < 2, blocks[j], blocks[j ^ 2]) for j in range(4)]
    total = jnp.concatenate(blocks, axis=1)
    return inv_row, dinv - total


def solution(mesh):
    in_specs = (P(), P(None, "prow", None), P("prow", "pcol"), P())
    out_specs = (P(None, None, "pcol"), P())
    return jax.shard_map(local, mesh=mesh, in_specs=in_specs, out_specs=out_specs, check_vma=False)
```
